256 devices in a mesh: sta: 64 (over y_lo, x, z), frq: 4 (over y_hi, core).
Axes of the slice: x: 4, y: 4 (y_hi: 2, y_lo: 2; y = y_hi * 2 + y_lo), z: 8, core: 2. Of those that a mesh axis runs over, the one named last changes fastest.
Arguments:
- traces: bfloat16 [1024, 32, 4096], P('sta', 'frq'), may hold values from -6 to 6
- gaps: int32 [1024, 32], P('sta', 'frq'), may hold values 0 or 1
- pair_mask: int32 [64, 64], replicated, may hold values 0 or 1
Outputs:
- stacked: bfloat16 [2, 1024, 1024, 512], P(None, 'sta', None, 'frq')
The draws below stay inside these ranges and needn't reach their ends.
All inputs are finite; a program needn't handle non-finite values. No bound on the sum of `gaps` on one device may be relied on, other than what follows from the above.
Results may differ from the reference program's by a relative error of at most 0.0069.
Values may be sent and summed in bfloat16 or wider, within the bound.
No kernel may reach another device: no remote copies, remote signals or barrier semaphores. Data moves between devices by JAX's collectives and lax.ppermute only.
A program may use at most 256 MiB of HBM per device.

```python
import math
import jax
import jax.numpy as jnp
from jax import lax

SAMPLES = 4096
BINS = 512
SMOOTH_HALF = 4
STA_DEV = 16
WINDOWS = 32
STATIONS = 1024
BLOCKS = 64
N_STA = 64


def with_ends(entries, own_key, low, top_value):
    spot = [jax.random.randint(jax.random.fold_in(own_key, axis), (), 0, length) for axis, length in enumerate(entries.shape)]
    main_axis = entries.shape.index(max(entries.shape))
    next_to = spot[:main_axis] + [(spot[main_axis] + 1) % entries.shape[main_axis]] + spot[main_axis + 1:]
    return entries.at[tuple(spot)].set(low).at[tuple(next_to)].set(top_value)


def levels(own_key, shape, cuts, least, top_value):
    def one(position, shards_of):
        heights = jax.random.uniform(jax.random.fold_in(jax.random.fold_in(own_key, 6), position), (shards_of,), jnp.float32, least / len(cuts), top_value / len(cuts))
        return jnp.repeat(jnp.exp(heights), shape[position] // shards_of).reshape((-1,) + (1,) * (len(shape) - position - 1))

    factor_of = one(*cuts[0])
    for cut in cuts[1:]:
        factor_of = factor_of * one(*cut)
    return factor_of


def gaussian(stream_key, dims, deviation, bound, cuts=(), kind=jnp.bfloat16):
    level = levels(stream_key, dims, cuts, -0.22, 0.18) if cuts else 1.0
    values = jax.random.normal(stream_key, dims, jnp.float32) * deviation * level
    return jnp.minimum(jnp.maximum(values, -bound), bound).astype(kind)


def setup_inputs(seed: int = 0) -> dict:
    arg_keys = jax.random.split(jax.random.key(seed), 4)
    return {
        "traces": gaussian(arg_keys[0], (STATIONS, WINDOWS, SAMPLES), 1.0, 6.0, ((0, 64), (1, 4))),
        "gaps": with_ends((jax.random.randint(arg_keys[1], (STATIONS, WINDOWS), 0, 8) < 7).astype(jnp.int32), jax.random.fold_in(arg_keys[1], 1), 0, 1),
        "pair_mask": with_ends((jax.random.randint(arg_keys[2], (BLOCKS, BLOCKS), 0, 4) < 3).astype(jnp.int32), jax.random.fold_in(arg_keys[2], 1), 0, 1),
    }


def basis_table(samples, bins):
    sample_ids = jnp.arange(samples, dtype=jnp.int32)
    bin_ids = jnp.arange(1, bins + 1, dtype=jnp.int32)
    phases = sample_ids[:, None] * bin_ids[None, :] % samples
    angles = 2.0 * math.pi / samples * phases.astype(jnp.float32)
    tapering = 0.5 - 0.5 * jnp.cos(2.0 * math.pi / samples * sample_ids.astype(jnp.float32))
    scaling = tapering[:, None] / math.sqrt(samples)
    return jnp.concatenate([scaling * jnp.cos(angles), -scaling * jnp.sin(angles)], 1).astype(jnp.bfloat16)

def whiten(spectrum, gaps, bins, half):
    real_part = spectrum[..., :bins]
    imag_part = spectrum[..., bins:]
    magnitude = jnp.sqrt(real_part * real_part + imag_part * imag_part)
    widths = [(0, 0)] * (magnitude.ndim - 1) + [(half, half)]
    padded = jnp.pad(magnitude, widths)
    ones_pad = jnp.pad(jnp.ones((bins,), jnp.float32), (half, half))
    summed = padded[..., 0:bins]
    counts = ones_pad[0:bins]
    for offset in range(1, 2 * half + 1):
        summed = summed + padded[..., offset:offset + bins]
        counts = counts + ones_pad[offset:offset + bins]
    smoothed = summed / counts
    level = lax.optimization_barrier(jnp.mean(magnitude, axis=-1, keepdims=True))
    factor = gaps.astype(jnp.float32)[..., None] / (smoothed + 0.1 * level + 1e-06)
    return jnp.stack([real_part * factor, imag_part * factor], -2).astype(jnp.bfloat16)

def reference(traces, gaps, pair_mask):
    stations = traces.shape[0]
    basis = basis_table(SAMPLES, BINS)
    spectrum = jnp.dot(traces.reshape(-1, SAMPLES), basis, preferred_element_type=jnp.float32)
    spectrum = spectrum.reshape(stations, WINDOWS, 2 * BINS)
    whitened = whiten(spectrum, gaps, BINS, SMOOTH_HALF)
    blocks = whitened.reshape(N_STA, STA_DEV, WINDOWS, 2, BINS)
    column_block = jnp.arange(stations, dtype=jnp.int32) // STA_DEV
    all_rows = whitened.astype(jnp.float32)

    def one_block(inputs):
        rows, block_id = inputs
        product = jnp.einsum('awcf,bwdf->cdabf', rows.astype(jnp.float32), all_rows)
        real_cross = product[0, 0] + product[1, 1]
        imag_cross = product[1, 0] - product[0, 1]
        mask_row = lax.dynamic_index_in_dim(pair_mask, block_id, 0, keepdims=False)
        mask_cols = mask_row[column_block].astype(jnp.float32)
        joined = jnp.stack([real_cross, imag_cross], 0)
        return (joined * (mask_cols / WINDOWS)[None, None, :, None]).astype(jnp.bfloat16)
    result = lax.map(one_block, (blocks, jnp.arange(N_STA, dtype=jnp.int32)))
    return jnp.transpose(result, (1, 0, 2, 3, 4)).reshape(2, stations, stations, BINS)
```

```python
import functools
import itertools
import math

import jax
import jax.numpy as jnp
import numpy as np
from jax import lax
from jax.experimental import pallas as pl
from jax.experimental.pallas import tpu as pltpu
from jax.sharding import PartitionSpec as P

SAMPLES = 4096
BINS = 512
HALF = 4
WINDOWS = 32
STATIONS = 16
LOCAL_WINDOWS = 8
SLABS = 4
SLAB_BINS = 128
GROUPS = 16
Y, X, Z = 2, 4, 8
COLUMN = Z * STATIONS
STEPS = 8
GSTEP = 4
VMEM_BYTES = 24 << 20


def basis_table():
    sample = np.arange(SAMPLES)
    bins = np.arange(1, BINS + 1)
    angle = (2.0 * math.pi / SAMPLES) * (sample[:, None] * bins[None, :] % SAMPLES)
    taper = 0.5 - 0.5 * np.cos((2.0 * math.pi / SAMPLES) * sample)
    scale = taper[:, None] / math.sqrt(SAMPLES)
    table = np.concatenate([scale * np.cos(angle), -scale * np.sin(angle)], 1)
    return table.astype(np.float32).astype(jnp.bfloat16)


def spectra_kernel(traces_ref, basis_ref, gaps_ref, out_ref, turned):
    rows = STATIONS * LOCAL_WINDOWS
    total = jnp.zeros((rows, 2 * BINS), jnp.float32)
    for step in range(STEPS):
        depth = slice(step * (SAMPLES // STEPS), (step + 1) * (SAMPLES // STEPS))
        total += jnp.dot(traces_ref[:, depth], basis_ref[depth], preferred_element_type=jnp.float32)
    real = total[:, :BINS]
    imag = total[:, BINS:]
    magnitude = jnp.sqrt(real * real + imag * imag)
    lane = lax.broadcasted_iota(jnp.int32, magnitude.shape, 1)
    summed = magnitude
    for offset in range(1, HALF + 1):
        after = pltpu.roll(magnitude, BINS - offset, 1)
        before = pltpu.roll(magnitude, offset, 1)
        summed = summed + jnp.where(lane < BINS - offset, after, 0.0)
        summed = summed + jnp.where(lane >= offset, before, 0.0)
    counts = 1 + jnp.minimum(lane, HALF) + jnp.minimum(BINS - 1 - lane, HALF)
    smoothed = summed / counts.astype(jnp.float32)
    level = jnp.sum(magnitude, axis=1, keepdims=True) / BINS
    spread = jnp.concatenate([gaps_ref[...]] * STATIONS, 0)
    station = lax.broadcasted_iota(jnp.int32, spread.shape, 0) // LOCAL_WINDOWS
    chosen = station == lax.broadcasted_iota(jnp.int32, spread.shape, 1)
    complete = jnp.sum(jnp.where(chosen, spread, 0), axis=1, keepdims=True)
    factor = complete.astype(jnp.float32) / (smoothed + 0.1 * level + 1e-06)
    bins = lax.broadcasted_iota(jnp.int32, (BINS, BINS), 0)
    lanes = lax.broadcasted_iota(jnp.int32, (BINS, BINS), 1)
    order = (bins % 4 * 2 + bins // 4 % 2) * 64 + bins // 8 == lanes
    order = jnp.where(order, 1.0, 0.0).astype(jnp.bfloat16)
    parts = []
    for part in (real, imag):
        white = (part * factor).astype(jnp.bfloat16)
        parts.append(jnp.dot(white, order, preferred_element_type=jnp.float32))
    for station in range(STATIONS):
        at = slice(station * LOCAL_WINDOWS, (station + 1) * LOCAL_WINDOWS)
        stacked = jnp.concatenate(
            [parts[c][at, pair * 128 : pair * 128 + 128] for pair in range(4) for c in range(2)], 0
        )
        flipped = stacked.T
        joined = jnp.concatenate([flipped[:64], flipped[64:]], 1)
        turned[pl.ds(station, 64, stride=STATIONS), :] = joined
    out_ref[...] = turned[...].astype(jnp.bfloat16)


def local_spectra(traces, gaps):
    rows = STATIONS * LOCAL_WINDOWS
    flat = pl.pallas_call(
        spectra_kernel,
        out_shape=jax.ShapeDtypeStruct((SLABS * GROUPS * STATIONS, 128), jnp.bfloat16),
        in_specs=[pl.BlockSpec(memory_space=pltpu.VMEM)] * 3,
        out_specs=pl.BlockSpec(memory_space=pltpu.VMEM),
        scratch_shapes=[pltpu.VMEM((SLABS * GROUPS * STATIONS, 128), jnp.float32)],
        compiler_params=pltpu.CompilerParams(vmem_limit_bytes=VMEM_BYTES),
        cost_estimate=pl.CostEstimate(flops=1 << 30, bytes_accessed=10 << 20, transcendentals=0),
        name="spectra",
    )(traces.reshape(rows, SAMPLES), jnp.asarray(basis_table()), gaps.T)
    return flat.reshape(SLABS, GROUPS, STATIONS, 128)


def rows_kernel(own_ref, out_ref):
    for g, part in itertools.product(range(GSTEP), range(SLABS)):
        own = own_ref[part, g].astype(jnp.float32)
        lane = lax.broadcasted_iota(jnp.int32, own.shape, 1)
        real = lane // 8 % 2 == 0
        crossed = jnp.where(real, pltpu.roll(own, 120, 1), -pltpu.roll(own, 8, 1))
        for c, rows in enumerate((own, crossed)):
            spread = jnp.broadcast_to(rows[:, None, :], (STATIONS, 8, 128))
            j = lax.broadcasted_iota(jnp.int32, spread.shape, 1)
            owner = lax.broadcasted_iota(jnp.int32, spread.shape, 2) // 16
            spread = jnp.where(j == owner, spread, 0.0).reshape(128, 128)
            out_ref[pl.program_id(0) * GSTEP + g, c * 128 : c * 128 + 128, part * 128 : part * 128 + 128] = spread.astype(jnp.bfloat16)


def own_rows(own):
    return pl.pallas_call(
        rows_kernel,
        grid=(GROUPS // GSTEP,),
        out_shape=jax.ShapeDtypeStruct((GROUPS, 256, 512), jnp.bfloat16),
        in_specs=[pl.BlockSpec((SLABS, GSTEP, STATIONS, 128), lambda g: (0, g, 0, 0))],
        out_specs=pl.BlockSpec(memory_space=pltpu.VMEM),
        compiler_params=pltpu.CompilerParams(vmem_limit_bytes=VMEM_BYTES),
        cost_estimate=pl.CostEstimate(flops=1 << 22, bytes_accessed=5 << 20, transcendentals=0),
        name="own_rows",
    )(own)


def cross_kernel(columns, where_ref, mask_ref, rows_ref, *refs):
    out_ref, products = refs[-2], refs[-1]
    step = pl.program_id(0)
    width = len(columns) * COLUMN

    @pl.when(step < GROUPS // GSTEP)
    def _():
        for g in range(GSTEP):
            others = jnp.concatenate(
                [
                    jnp.concatenate([refs[piece][(*at, part, g)] for column in columns for piece, *at in column], 0)
                    for part in range(SLABS)
                ],
                1,
            )
            product = lax.dot_general(
                rows_ref[step * GSTEP + g], others, (((1,), (1,)), ((), ())), preferred_element_type=jnp.float32
            )
            first = pl.multiple_of(step * (GSTEP * 8) + g * 8, 8)
            products[:, pl.ds(first, 8), :] = product.reshape(32, 8, width)

    for n in range(len(columns)):

        @pl.when(step == GROUPS // GSTEP - 1 + n)
        def _():
            shift = where_ref[2 * n + 1]
            for c, a in itertools.product(range(2), range(STATIONS)):
                turned = products[c * STATIONS + a, :, n * COLUMN : (n + 1) * COLUMN].T
                for k in range(Z):
                    first = pl.multiple_of(lax.rem(shift + k, Z) * STATIONS, STATIONS)
                    block = turned[k * STATIONS : k * STATIONS + STATIONS] * mask_ref[pl.ds(first, STATIONS), :]
                    out_ref[c, a, pl.ds(first, STATIONS), :] = block.astype(jnp.bfloat16)


def cross(out, where, rows, mask, pieces, columns):
    steps = GROUPS // GSTEP

    def number(i, w):
        return w[2 * jnp.maximum(i - (steps - 1), 0)]

    in_specs = [
        pl.BlockSpec((COLUMN, 128), lambda i, w: (number(i, w), 0)),
        pl.BlockSpec(memory_space=pltpu.VMEM),
    ]
    for piece in pieces:
        lead = piece.shape[:-4]
        zeros = (0,) * (len(lead) + 1)
        in_specs.append(
            pl.BlockSpec(
                (*lead, SLABS, GSTEP, STATIONS, 128),
                lambda i, w, zeros=zeros: (*zeros, jnp.minimum(i, steps - 1), 0, 0),
            )
        )
    args = [jnp.concatenate(where), mask, rows, *pieces]
    aliases = {}
    if out is not None:
        in_specs.append(pl.BlockSpec(memory_space=pl.ANY))
        aliases = {len(args): 0}
        args.append(out)
    stations = Y * X * COLUMN
    n = len(columns)
    return pl.pallas_call(
        functools.partial(cross_kernel, columns),
        grid_spec=pltpu.PrefetchScalarGridSpec(
            num_scalar_prefetch=1,
            grid=(steps + n - 1,),
            in_specs=in_specs,
            out_specs=pl.BlockSpec((2, STATIONS, COLUMN, SLAB_BINS), lambda i, w: (0, 0, number(i, w), 0)),
            scratch_shapes=[pltpu.VMEM((2 * STATIONS, SLAB_BINS, n * COLUMN), jnp.float32)],
        ),
        out_shape=jax.ShapeDtypeStruct((2, STATIONS, stations, SLAB_BINS), jnp.bfloat16),
        input_output_aliases=aliases,
        compiler_params=pltpu.CompilerParams(vmem_limit_bytes=VMEM_BYTES),
        cost_estimate=pl.CostEstimate(
            flops=n << 32, bytes_accessed=(4 + 3 * n) << 20, transcendentals=0
        ),
        name="cross",
    )(*args)


def place(y, x, z):
    return (y % Y) * X * Z + (x % X) * Z + z


def moved(value, dy=0, dx=0, dz=0):
    perm = [
        (place(y + dy, x + dx, (z + dz) % Z), place(y, x, z))
        for y in range(Y)
        for x in range(X)
        for z in range(Z)
    ]
    return lax.ppermute(value, "sta", perm)


Z_GROUPS = [[place(y, x, z) for z in range(Z)] for y in range(Y) for x in range(X)]

RING = ((0, 0), (0, 1), (1, 0), (1, 2), (1, 4), (1, 3), (1, 1), (0, 2))


def after(value, *others):
    return lax.optimization_barrier((value, *others))[0]


def per_device(traces, gaps, pair_mask):
    local = local_spectra(traces, gaps)
    own = lax.all_to_all(local, "frq", split_axis=0, concat_axis=0, tiled=True)[None]
    device = lax.axis_index("sta")
    y, x, z = device // (X * Z), device // Z % X, device % Z
    own_row = lax.dynamic_index_in_dim(pair_mask, device, 0, keepdims=False)
    scale = jnp.repeat(own_row.astype(jnp.float32) / WINDOWS, STATIONS)
    mask = jnp.broadcast_to(scale[:, None], (Y * X * COLUMN, 128))

    def where(dy, dx, first):
        return jnp.stack([(y + dy) % Y * X + (x + dx) % X, first]).astype(jnp.int32)

    up1, down1 = moved(own, dz=1), moved(own, dz=-1)
    s10 = moved(own, dy=1)
    rows = own_rows(own[0])
    s10 = after(s10, up1, down1)
    up2, down2 = moved(up1, dz=1), moved(down1, dz=-1)
    s11, s13 = moved(s10, dx=1), moved(s10, dx=-1)
    near = jnp.concatenate([own, up1, down1], 0)
    n10, n01, n03 = moved(near, dy=1), moved(near, dx=1), moved(near, dx=-1)
    s11 = after(s11, up2, down2)
    up3, down3 = moved(up2, dz=1), moved(down2, dz=-1)
    s12 = moved(s11, dx=1)
    low = moved(up3[:, :2], dz=1)
    high = moved(down3[:, 2:], dz=-1)
    seeds = jnp.concatenate([s11, s13, after(s12, up3, down3)], 0)
    far = lax.all_gather(seeds.reshape(-1, 128), "sta", axis_index_groups=Z_GROUPS)
    far = far.reshape(Z, 3, SLABS, GROUPS, STATIONS, 128)
    last = jnp.concatenate([up2, down2, up3, down3, jnp.concatenate([low, high], 1)], 0)
    l10, l01, l03 = moved(last, dy=1), moved(last, dx=1), moved(last, dx=-1)
    c02 = [moved(n01, dx=1), moved(l03[:4], dx=-1), moved(l01[4:], dx=1)]

    def ring(first):
        return tuple((first + piece, k) for piece, k in RING)

    out = cross(None, [where(0, 0, z)], rows, mask, [near, last], (ring(0),))
    out = cross(
        out,
        [where(1, 0, z), where(0, 1, z), where(0, 3, z)],
        rows,
        mask,
        [n10, l10, n01, l01, n03, l03],
        (ring(0), ring(2), ring(4)),
    )
    order = tuple((2, 0) if (piece, k) == (1, 4) else (piece, k) for piece, k in RING)
    out = cross(out, [where(0, 2, z)], rows, mask, c02, (order,))
    return cross(
        out,
        [where(1, dx, 0 * z) for dx in (1, 3, 2)],
        rows,
        mask,
        [far],
        tuple(tuple((0, k, n) for k in range(Z)) for n in range(3)),
    )


def solution(mesh):
    return jax.shard_map(
        per_device,
        mesh=mesh,
        in_specs=(P("sta", "frq", None), P("sta", "frq"), P()),
        out_specs=P(None, "sta", None, "frq"),
        check_vma=False,
    )
```

```python
import functools
import itertools
import math

import jax
import jax.numpy as jnp
import numpy as np
from jax import lax
from jax.experimental import pallas as pl
from jax.experimental.pallas import tpu as pltpu
from jax.sharding import PartitionSpec as P

SAMPLES = 4096
BINS = 512
HALF = 4
WINDOWS = 32
STATIONS = 16
LOCAL_WINDOWS = 8
SLABS = 4
SLAB_BINS = 128
GROUPS = 16
Y, X, Z = 2, 4, 8
COLUMN = Z * STATIONS
STEPS = 8
GSTEP = 4
CROSS_STEPS = GROUPS // GSTEP
VMEM_BYTES = 24 << 20


def basis_table():
    sample = np.arange(SAMPLES)
    bins = np.arange(1, BINS + 1)
    angle = (2.0 * math.pi / SAMPLES) * (sample[:, None] * bins[None, :] % SAMPLES)
    taper = 0.5 - 0.5 * np.cos((2.0 * math.pi / SAMPLES) * sample)
    scale = taper[:, None] / math.sqrt(SAMPLES)
    table = np.concatenate([scale * np.cos(angle), -scale * np.sin(angle)], 1)
    return table.astype(np.float32).astype(jnp.bfloat16)


def spectra_kernel(traces_ref, basis_ref, gaps_ref, out_ref, turned, traces_here, basis_here, done):
    rows = STATIONS * LOCAL_WINDOWS
    total = jnp.zeros((rows, 2 * BINS), jnp.float32)
    copies = [pltpu.make_async_copy(traces_ref, traces_here, done.at[STEPS])]
    parts = []
    for step in range(STEPS):
        depth = pl.ds(step * (SAMPLES // STEPS), SAMPLES // STEPS)
        parts.append(depth)
        copies.append(pltpu.make_async_copy(basis_ref.at[depth], basis_here.at[depth], done.at[step]))
    for copy in copies:
        copy.start()
    copies[0].wait()
    for depth, copy in zip(parts, copies[1:]):
        copy.wait()
        total += jnp.dot(traces_here[:, depth], basis_here[depth], preferred_element_type=jnp.float32)
    real = total[:, :BINS]
    imag = total[:, BINS:]
    magnitude = jnp.sqrt(real * real + imag * imag)
    lane = lax.broadcasted_iota(jnp.int32, magnitude.shape, 1)
    summed = magnitude
    for offset in range(1, HALF + 1):
        after = pltpu.roll(magnitude, BINS - offset, 1)
        before = pltpu.roll(magnitude, offset, 1)
        summed = summed + jnp.where(lane < BINS - offset, after, 0.0)
        summed = summed + jnp.where(lane >= offset, before, 0.0)
    counts = 1 + jnp.minimum(lane, HALF) + jnp.minimum(BINS - 1 - lane, HALF)
    smoothed = summed / counts.astype(jnp.float32)
    level = jnp.sum(magnitude, axis=1, keepdims=True) / BINS
    spread = jnp.concatenate([gaps_ref[...]] * STATIONS, 0)
    station = lax.broadcasted_iota(jnp.int32, spread.shape, 0) // LOCAL_WINDOWS
    chosen = station == lax.broadcasted_iota(jnp.int32, spread.shape, 1)
    complete = jnp.sum(jnp.where(chosen, spread, 0), axis=1, keepdims=True)
    factor = complete.astype(jnp.float32) / (smoothed + 0.1 * level + 1e-06)
    bins = lax.broadcasted_iota(jnp.int32, (BINS, BINS), 0)
    lanes = lax.broadcasted_iota(jnp.int32, (BINS, BINS), 1)
    order = (bins % 4 * 2 + bins // 4 % 2) * 64 + bins // 8 == lanes
    order = jnp.where(order, 1.0, 0.0).astype(jnp.bfloat16)
    parts = []
    for part in (real, imag):
        white = (part * factor).astype(jnp.bfloat16)
        parts.append(jnp.dot(white, order, preferred_element_type=jnp.float32))
    for station in range(STATIONS):
        at = slice(station * LOCAL_WINDOWS, (station + 1) * LOCAL_WINDOWS)
        stacked = jnp.concatenate(
            [parts[c][at, pair * 128 : pair * 128 + 128] for pair in range(4) for c in range(2)], 0
        )
        flipped = stacked.T
        joined = jnp.concatenate([flipped[:64], flipped[64:]], 1)
        turned[pl.ds(station, 64, stride=STATIONS), :] = joined
    out_ref[...] = turned[...].astype(jnp.bfloat16)


def local_spectra(traces, gaps):
    rows = STATIONS * LOCAL_WINDOWS
    flat = pl.pallas_call(
        spectra_kernel,
        out_shape=jax.ShapeDtypeStruct((SLABS * GROUPS * STATIONS, 128), jnp.bfloat16),
        in_specs=[
            pl.BlockSpec(memory_space=pl.ANY),
            pl.BlockSpec(memory_space=pl.ANY),
            pl.BlockSpec(memory_space=pltpu.VMEM),
        ],
        out_specs=pl.BlockSpec(memory_space=pltpu.VMEM),
        scratch_shapes=[
            pltpu.VMEM((SLABS * GROUPS * STATIONS, 128), jnp.float32),
            pltpu.VMEM((rows, SAMPLES), jnp.bfloat16),
            pltpu.VMEM((SAMPLES, 2 * BINS), jnp.bfloat16),
            pltpu.SemaphoreType.DMA((STEPS + 1,)),
        ],
        compiler_params=pltpu.CompilerParams(vmem_limit_bytes=60 << 20),
        cost_estimate=pl.CostEstimate(flops=1 << 30, bytes_accessed=10 << 20, transcendentals=0),
        name="spectra",
    )(traces.reshape(rows, SAMPLES), jnp.asarray(basis_table()), gaps.T)
    return flat.reshape(SLABS, GROUPS, STATIONS, 128)


def rows_kernel(own_ref, out_ref):
    for g, part in itertools.product(range(GSTEP), range(SLABS)):
        own = own_ref[part, g].astype(jnp.float32)
        lane = lax.broadcasted_iota(jnp.int32, own.shape, 1)
        real = lane // 8 % 2 == 0
        crossed = jnp.where(real, pltpu.roll(own, 120, 1), -pltpu.roll(own, 8, 1))
        for c, rows in enumerate((own, crossed)):
            spread = jnp.broadcast_to(rows[:, None, :], (STATIONS, 8, 128))
            j = lax.broadcasted_iota(jnp.int32, spread.shape, 1)
            owner = lax.broadcasted_iota(jnp.int32, spread.shape, 2) // 16
            spread = jnp.where(j == owner, spread, 0.0).reshape(128, 128)
            out_ref[pl.program_id(0) * GSTEP + g, c * 128 : c * 128 + 128, part * 128 : part * 128 + 128] = spread.astype(jnp.bfloat16)


def own_rows(own):
    return pl.pallas_call(
        rows_kernel,
        grid=(GROUPS // GSTEP,),
        out_shape=jax.ShapeDtypeStruct((GROUPS, 256, 512), jnp.bfloat16),
        in_specs=[pl.BlockSpec((SLABS, GSTEP, STATIONS, 128), lambda g: (0, g, 0, 0))],
        out_specs=pl.BlockSpec(memory_space=pltpu.VMEM),
        compiler_params=pltpu.CompilerParams(vmem_limit_bytes=VMEM_BYTES),
        cost_estimate=pl.CostEstimate(flops=1 << 22, bytes_accessed=5 << 20, transcendentals=0),
        name="own_rows",
    )(own)


def cross_kernel(columns, split, turned, where_ref, mask_ref, rows_ref, *refs):
    out_ref, products = refs[-2], refs[-1]
    step = pl.program_id(0)
    width = len(columns) * COLUMN

    def multiply(late):
        scale = jnp.concatenate([mask_ref[pl.ds(where_ref[3 * n + 2], 1), :] for n in range(len(columns))], 1)
        halves = []
        for g in range(GSTEP):
            others = jnp.concatenate(
                [
                    jnp.concatenate(
                        [
                            column(refs, k, part, g, late, where_ref[3 * n + 1])
                            for n, column in enumerate(columns)
                            for k in range(Z)
                        ],
                        0,
                    )
                    for part in range(SLABS)
                ],
                1,
            )
            product = lax.dot_general(
                rows_ref[step * GSTEP + g], others, (((1,), (1,)), ((), ())), preferred_element_type=jnp.float32
            )
            halves.append((product * scale).reshape(32, 8, width))
            if g % 2:
                first = pl.multiple_of(step * (GSTEP * 8) + (g - 1) * 8, 16)
                products[:, pl.ds(first, 16), :] = jnp.concatenate(halves, 1).astype(jnp.bfloat16)
                halves = []

    if split:
        pl.when(step < CROSS_STEPS // 2)(lambda: multiply(False))
        pl.when((step >= CROSS_STEPS // 2) & (step < CROSS_STEPS))(lambda: multiply(True))
    else:
        pl.when(step < CROSS_STEPS)(lambda: multiply(False))

    for n in range(len(columns)):

        @pl.when(step == CROSS_STEPS - 1 + n)
        def _():
            shift = where_ref[3 * n + 1]
            for c, a in itertools.product(range(2), range(STATIONS)):
                block = products[c * STATIONS + a, :, n * COLUMN : (n + 1) * COLUMN].T
                if not turned[n]:
                    out_ref[c, a] = block
                    continue
                for k in range(Z):
                    first = pl.multiple_of(lax.rem(shift + k, Z) * STATIONS, STATIONS)
                    out_ref[c, a, pl.ds(first, STATIONS), :] = block[k * STATIONS : k * STATIONS + STATIONS]


def cross(out, turned, where, rows, mask, pieces, columns, split=False, vmem_bytes=VMEM_BYTES):
    def number(i, w):
        return w[3 * jnp.maximum(i - (CROSS_STEPS - 1), 0)]

    in_specs = [pl.BlockSpec(memory_space=pltpu.VMEM), pl.BlockSpec(memory_space=pltpu.VMEM)]
    for _, block, at in pieces:
        in_specs.append(pl.BlockSpec(block, lambda i, w, at=at: at(jnp.minimum(i, CROSS_STEPS - 1))))
    args = [jnp.concatenate(where), mask, rows, *[piece for piece, _, _ in pieces]]
    aliases = {}
    if out is not None:
        in_specs.append(pl.BlockSpec(memory_space=pl.ANY))
        aliases = {len(args): 0}
        args.append(out)
    stations = Y * X * COLUMN
    n = len(columns)
    return pl.pallas_call(
        functools.partial(cross_kernel, columns, split, turned),
        grid_spec=pltpu.PrefetchScalarGridSpec(
            num_scalar_prefetch=1,
            grid=(CROSS_STEPS + n - 1,),
            in_specs=in_specs,
            out_specs=pl.BlockSpec((2, STATIONS, COLUMN, SLAB_BINS), lambda i, w: (0, 0, number(i, w), 0)),
            scratch_shapes=[pltpu.VMEM((2 * STATIONS, SLAB_BINS, n * COLUMN), jnp.bfloat16)],
        ),
        out_shape=jax.ShapeDtypeStruct((2, STATIONS, stations, SLAB_BINS), jnp.bfloat16),
        input_output_aliases=aliases,
        compiler_params=pltpu.CompilerParams(vmem_limit_bytes=vmem_bytes),
        cost_estimate=pl.CostEstimate(
            flops=n << 29, bytes_accessed=1, transcendentals=0
        ),
        name="cross",
    )(*args)


def whole(piece):
    block = (piece.shape[0], SLABS, GSTEP, STATIONS, 128)
    last = piece.shape[2] // GSTEP - 1
    return piece, block, lambda i: (0, 0, jnp.minimum(i, last), 0, 0)


def ring(first, order):
    def read(refs, k, part, g, late, shift):
        piece, position = order[k]
        return refs[first + piece][position, part, g]

    return read


def place(y, x, z):
    return (y % Y) * X * Z + (x % X) * Z + z


def moved(value, dy=0, dx=0, dz=0):
    perm = [
        (place(y + dy, x + dx, (z + dz) % Z), place(y, x, z))
        for y in range(Y)
        for x in range(X)
        for z in range(Z)
    ]
    return lax.ppermute(value, "sta", perm)


Z_GROUPS = [[place(y, x, z) for z in range(Z)] for y in range(Y) for x in range(X)]

RING = ((0, 0), (1, 0), (2, 0), (3, 0), (3, 2), (3, 1), (2, 1), (1, 1))


def after(value, *others):
    return lax.optimization_barrier((value, *others))[0]


def per_device(traces, gaps, pair_mask):
    local = local_spectra(traces, gaps)
    own = lax.all_to_all(local, "frq", split_axis=0, concat_axis=0, tiled=True)[None]
    device = lax.axis_index("sta")
    y, x, z = device // (X * Z), device // Z % X, device % Z
    own_row = lax.dynamic_index_in_dim(pair_mask, device, 0, keepdims=False)
    scale = own_row.astype(jnp.float32).reshape(Y * X, Z) / WINDOWS
    turned = lax.dynamic_slice_in_dim(jnp.concatenate([scale, scale], 1), z, Z, 1)
    mask = jnp.repeat(jnp.concatenate([scale, turned], 0), STATIONS, 1)

    def where(dy, dx, ring):
        column = (y + dy) % Y * X + (x + dx) % X
        return jnp.stack([column, z, column + Y * X] if ring else [column, 0 * z, column]).astype(jnp.int32)

    early = slice(None, GROUPS // 2)
    up1, down1 = moved(own, dz=1), moved(own, dz=-1)
    s01, s03 = moved(own, dx=1), moved(own, dx=-1)
    s10 = moved(own, dy=1)
    rows = own_rows(own[0])
    up1, down1 = lax.optimization_barrier((up1, down1, s10))[:2]
    up2, down2 = moved(up1, dz=1), moved(down1, dz=-1)
    s02 = moved(s01, dx=1)
    beside = moved(jnp.concatenate([s03, s01], 0), dy=1)
    s13, s11 = beside[:1], beside[1:]
    s12 = moved(s02, dy=1)
    near = jnp.concatenate([up1, down1], 0)
    n03 = moved(near, dx=-1)
    n01 = moved(after(near, s02), dx=1)
    n10 = moved(after(near, s12), dy=1)
    up3, down3 = moved(up2, dz=1), moved(down2, dz=-1)
    seeds = [s13, s12, s11[:, :, GROUPS // 2 :]]
    seeds = after(jnp.concatenate([seed.reshape(-1, 128) for seed in seeds], 0), up3, down3, n01, n03)
    far = lax.all_gather(seeds, "sta", axis_index_groups=Z_GROUPS)
    far = far.reshape(Z, 10, GROUPS, STATIONS, 128)
    low = moved(up3[:, :2], dz=1)
    high = moved(down3[:, 2:], dz=-1)
    middle = after(jnp.concatenate([up2, down2], 0), low, high, n10)
    m10, m01, m03 = moved(middle, dy=1), moved(middle, dx=1), moved(middle, dx=-1)
    last = jnp.concatenate([up3, down3, jnp.concatenate([low, high], 1)], 0)
    last = after(last, m01, m03, m10)
    l10, l01, l03 = moved(last, dy=1), moved(last, dx=1), moved(last, dx=-1)
    n02, m02 = moved(n01, dx=1), moved(m03, dx=-1)
    pieces = [whole(p) for p in (own, near, middle, last)]
    out = cross(None, (True,), [where(0, 0, True)], rows, mask, pieces, (ring(0, RING),))
    out, l01, l03 = lax.optimization_barrier((out, l01, l03))
    n11, m11, l11 = [moved(piece[:, :, early], dy=1) for piece in (n01, m01, l01)]
    c02 = [s02, n02, m02, moved(l03[:2], dx=-1), moved(l01[2:], dx=1)]
    out = cross(
        out,
        (True, True, True),
        [where(1, 0, True), where(0, 1, True), where(0, 3, True)],
        rows,
        mask,
        [whole(p) for p in (s10, n10, m10, l10, s01, n01, m01, l01, s03, n03, m03, l03)],
        (ring(0, RING), ring(4, RING), ring(8, RING)),
    )
    order = tuple((4, 0) if (piece, k) == (3, 2) else (piece, k) for piece, k in RING)
    out = cross(out, (True,), [where(0, 2, True)], rows, mask, [whole(p) for p in c02], (ring(0, order),))
    half = CROSS_STEPS // 2
    pieces = [
        (far, (Z, 2 * SLABS, GSTEP, STATIONS, 128), lambda i: (0, 0, i, 0, 0)),
        (far, (Z, 2, GSTEP, STATIONS, 128), lambda i: (0, SLABS, jnp.maximum(i - half, 0), 0, 0)),
        (far, (Z, 2, GSTEP, STATIONS, 128), lambda i: (0, SLABS, jnp.maximum(i, half), 0, 0)),
        *[whole(p) for p in (s11[:, :, early], n11, m11, l11)],
    ]

    def gathered(n):
        return lambda refs, k, part, g, late, shift: refs[0][k, n * SLABS + part, g]

    def mixed(refs, k, part, g, late, shift):
        if late:
            return refs[1 + part % 2][lax.rem(shift + k, Z), part // 2, g]
        return ring(3, RING)(refs, k, part, g, late, shift)

    return cross(
        out,
        (False, False, True),
        [where(1, 3, False), where(1, 2, False), where(1, 1, True)],
        rows,
        mask,
        pieces,
        (gathered(0), gathered(1), mixed),
        True,
        57 << 20,
    )


def solution(mesh):
    return jax.shard_map(
        per_device,
        mesh=mesh,
        in_specs=(P("sta", "frq", None), P("sta", "frq"), P()),
        out_specs=P(None, "sta", None, "frq"),
        check_vma=False,
    )
```

```python
import functools
import itertools
import math

import jax
import jax.numpy as jnp
import numpy as np
from jax import lax
from jax.experimental import pallas as pl
from jax.experimental.pallas import tpu as pltpu
from jax.sharding import PartitionSpec as P

SAMPLES = 4096
BINS = 512
HALF = 4
WINDOWS = 32
STATIONS = 16
LOCAL_WINDOWS = 8
SLABS = 4
SLAB_BINS = 128
GROUPS = 16
Y, X, Z = 2, 4, 8
COLUMN = Z * STATIONS
STEPS = 8
GSTEP = 4
CROSS_STEPS = GROUPS // GSTEP
VMEM_BYTES = 24 << 20
CROSS_VMEM_BYTES = 57 << 20


def basis_table():
    sample = np.arange(SAMPLES)
    bins = np.arange(1, BINS + 1)
    angle = (2.0 * math.pi / SAMPLES) * (sample[:, None] * bins[None, :] % SAMPLES)
    taper = 0.5 - 0.5 * np.cos((2.0 * math.pi / SAMPLES) * sample)
    scale = taper[:, None] / math.sqrt(SAMPLES)
    table = np.concatenate([scale * np.cos(angle), -scale * np.sin(angle)], 1)
    return table.astype(np.float32).astype(jnp.bfloat16)


def spectra_kernel(traces_ref, basis_ref, gaps_ref, out_ref, turned, traces_here, basis_here, done):
    rows = STATIONS * LOCAL_WINDOWS
    total = jnp.zeros((rows, 2 * BINS), jnp.float32)
    copies = [pltpu.make_async_copy(traces_ref, traces_here, done.at[STEPS])]
    parts = []
    for step in range(STEPS):
        depth = pl.ds(step * (SAMPLES // STEPS), SAMPLES // STEPS)
        parts.append(depth)
        copies.append(pltpu.make_async_copy(basis_ref.at[depth], basis_here.at[depth], done.at[step]))
    for copy in copies:
        copy.start()
    copies[0].wait()
    for depth, copy in zip(parts, copies[1:]):
        copy.wait()
        total += jnp.dot(traces_here[:, depth], basis_here[depth], preferred_element_type=jnp.float32)
    real = total[:, :BINS]
    imag = total[:, BINS:]
    magnitude = jnp.sqrt(real * real + imag * imag)
    lane = lax.broadcasted_iota(jnp.int32, magnitude.shape, 1)
    summed = magnitude
    for offset in range(1, HALF + 1):
        after = pltpu.roll(magnitude, BINS - offset, 1)
        before = pltpu.roll(magnitude, offset, 1)
        summed = summed + jnp.where(lane < BINS - offset, after, 0.0)
        summed = summed + jnp.where(lane >= offset, before, 0.0)
    counts = 1 + jnp.minimum(lane, HALF) + jnp.minimum(BINS - 1 - lane, HALF)
    smoothed = summed / counts.astype(jnp.float32)
    level = jnp.sum(magnitude, axis=1, keepdims=True) / BINS
    spread = jnp.concatenate([gaps_ref[...]] * STATIONS, 0)
    station = lax.broadcasted_iota(jnp.int32, spread.shape, 0) // LOCAL_WINDOWS
    chosen = station == lax.broadcasted_iota(jnp.int32, spread.shape, 1)
    complete = jnp.sum(jnp.where(chosen, spread, 0), axis=1, keepdims=True)
    factor = complete.astype(jnp.float32) / (smoothed + 0.1 * level + 1e-06)
    bins = lax.broadcasted_iota(jnp.int32, (BINS, BINS), 0)
    lanes = lax.broadcasted_iota(jnp.int32, (BINS, BINS), 1)
    order = (bins % 4 * 2 + bins // 4 % 2) * 64 + bins // 8 == lanes
    order = jnp.where(order, 1.0, 0.0).astype(jnp.bfloat16)
    parts = []
    for part in (real, imag):
        white = (part * factor).astype(jnp.bfloat16)
        parts.append(jnp.dot(white, order, preferred_element_type=jnp.float32))
    for station in range(STATIONS):
        at = slice(station * LOCAL_WINDOWS, (station + 1) * LOCAL_WINDOWS)
        stacked = jnp.concatenate(
            [parts[c][at, pair * 128 : pair * 128 + 128] for pair in range(4) for c in range(2)], 0
        )
        flipped = stacked.T
        joined = jnp.concatenate([flipped[:64], flipped[64:]], 1)
        turned[pl.ds(station, 64, stride=STATIONS), :] = joined
    out_ref[...] = turned[...].astype(jnp.bfloat16)


def local_spectra(traces, gaps):
    rows = STATIONS * LOCAL_WINDOWS
    flat = pl.pallas_call(
        spectra_kernel,
        out_shape=jax.ShapeDtypeStruct((SLABS * GROUPS * STATIONS, 128), jnp.bfloat16),
        in_specs=[
            pl.BlockSpec(memory_space=pl.ANY),
            pl.BlockSpec(memory_space=pl.ANY),
            pl.BlockSpec(memory_space=pltpu.VMEM),
        ],
        out_specs=pl.BlockSpec(memory_space=pltpu.VMEM),
        scratch_shapes=[
            pltpu.VMEM((SLABS * GROUPS * STATIONS, 128), jnp.float32),
            pltpu.VMEM((rows, SAMPLES), jnp.bfloat16),
            pltpu.VMEM((SAMPLES, 2 * BINS), jnp.bfloat16),
            pltpu.SemaphoreType.DMA((STEPS + 1,)),
        ],
        compiler_params=pltpu.CompilerParams(vmem_limit_bytes=60 << 20),
        cost_estimate=pl.CostEstimate(flops=1 << 30, bytes_accessed=10 << 20, transcendentals=0),
        name="spectra",
    )(traces.reshape(rows, SAMPLES), jnp.asarray(basis_table()), gaps.T)
    return flat.reshape(SLABS, GROUPS, STATIONS, 128)


def rows_kernel(own_ref, out_ref):
    for g, part in itertools.product(range(GSTEP), range(SLABS)):
        own = own_ref[part, g].astype(jnp.float32)
        lane = lax.broadcasted_iota(jnp.int32, own.shape, 1)
        real = lane // 8 % 2 == 0
        crossed = jnp.where(real, pltpu.roll(own, 120, 1), -pltpu.roll(own, 8, 1))
        for c, rows in enumerate((own, crossed)):
            spread = jnp.broadcast_to(rows[:, None, :], (STATIONS, 8, 128))
            j = lax.broadcasted_iota(jnp.int32, spread.shape, 1)
            owner = lax.broadcasted_iota(jnp.int32, spread.shape, 2) // 16
            spread = jnp.where(j == owner, spread, 0.0).reshape(128, 128)
            out_ref[pl.program_id(0) * GSTEP + g, c * 128 : c * 128 + 128, part * 128 : part * 128 + 128] = spread.astype(jnp.bfloat16)


def own_rows(own):
    return pl.pallas_call(
        rows_kernel,
        grid=(GROUPS // GSTEP,),
        out_shape=jax.ShapeDtypeStruct((GROUPS, 256, 512), jnp.bfloat16),
        in_specs=[pl.BlockSpec((SLABS, GSTEP, STATIONS, 128), lambda g: (0, g, 0, 0))],
        out_specs=pl.BlockSpec(memory_space=pltpu.VMEM),
        compiler_params=pltpu.CompilerParams(vmem_limit_bytes=VMEM_BYTES),
        cost_estimate=pl.CostEstimate(flops=1 << 22, bytes_accessed=5 << 20, transcendentals=0),
        name="own_rows",
    )(own)


def cross_kernel(base, columns, split, turned, where_ref, mask_ref, rows_ref, *refs):
    out_ref, products = refs[-2], refs[-1]
    step = pl.program_id(0)
    width = len(columns) * COLUMN

    def multiply(late):
        scale = jnp.concatenate([mask_ref[pl.ds(where_ref[3 * (base + n) + 2], 1), :] for n in range(len(columns))], 1)
        halves = []
        for g in range(GSTEP):
            others = jnp.concatenate(
                [
                    jnp.concatenate(
                        [
                            column(refs, k, part, g, late, where_ref[3 * (base + n) + 1])
                            for n, column in enumerate(columns)
                            for k in range(Z)
                        ],
                        0,
                    )
                    for part in range(SLABS)
                ],
                1,
            )
            product = lax.dot_general(
                rows_ref[step * GSTEP + g], others, (((1,), (1,)), ((), ())), preferred_element_type=jnp.float32
            )
            halves.append((product * scale).reshape(32, 8, width))
            if g % 2:
                first = pl.multiple_of(step * (GSTEP * 8) + (g - 1) * 8, 16)
                products[:, pl.ds(first, 16), :] = jnp.concatenate(halves, 1).astype(jnp.bfloat16)
                halves = []

    if split:
        pl.when(step < CROSS_STEPS // 2)(lambda: multiply(False))
        pl.when((step >= CROSS_STEPS // 2) & (step < CROSS_STEPS))(lambda: multiply(True))
    else:
        pl.when(step < CROSS_STEPS)(lambda: multiply(False))

    for n in range(len(columns)):

        @pl.when(step == CROSS_STEPS - 1 + n)
        def _():
            shift = where_ref[3 * (base + n) + 1]
            for c, a in itertools.product(range(2), range(STATIONS)):
                block = products[c * STATIONS + a, :, n * COLUMN : (n + 1) * COLUMN].T
                if not turned[n]:
                    out_ref[c, a] = block
                    continue
                for k in range(Z):
                    first = pl.multiple_of(lax.rem(shift + k, Z) * STATIONS, STATIONS)
                    out_ref[c, a, pl.ds(first, STATIONS), :] = block[k * STATIONS : k * STATIONS + STATIONS]


def cross(out, base, where, rows, mask, pieces, columns, split=False):
    def number(i, w):
        return w[3 * (base + jnp.maximum(i - (CROSS_STEPS - 1), 0))]

    in_specs = [pl.BlockSpec(memory_space=pltpu.VMEM), pl.BlockSpec(memory_space=pltpu.VMEM)]
    for _, block, at in pieces:
        in_specs.append(pl.BlockSpec(block, lambda i, w, at=at: at(jnp.minimum(i, CROSS_STEPS - 1))))
    args = [where, mask, rows, *[piece for piece, _, _ in pieces]]
    aliases = {}
    if out is not None:
        in_specs.append(pl.BlockSpec(memory_space=pl.ANY))
        aliases = {len(args): 0}
        args.append(out)
    stations = Y * X * COLUMN
    n = len(columns)
    turned = [first for _, _, first in COLUMNS[base : base + n]]
    return pl.pallas_call(
        functools.partial(cross_kernel, base, columns, split, turned),
        grid_spec=pltpu.PrefetchScalarGridSpec(
            num_scalar_prefetch=1,
            grid=(CROSS_STEPS + n - 1,),
            in_specs=in_specs,
            out_specs=pl.BlockSpec((2, STATIONS, COLUMN, SLAB_BINS), lambda i, w: (0, 0, number(i, w), 0)),
            scratch_shapes=[pltpu.VMEM((2 * STATIONS, SLAB_BINS, n * COLUMN), jnp.bfloat16)],
        ),
        out_shape=jax.ShapeDtypeStruct((2, STATIONS, stations, SLAB_BINS), jnp.bfloat16),
        input_output_aliases=aliases,
        compiler_params=pltpu.CompilerParams(vmem_limit_bytes=CROSS_VMEM_BYTES),
        cost_estimate=pl.CostEstimate(
            flops=n << 29, bytes_accessed=1, transcendentals=0
        ),
        name="cross",
    )(*args)


def whole(piece):
    block = (piece.shape[0], SLABS, GSTEP, STATIONS, 128)
    last = piece.shape[2] // GSTEP - 1
    return piece, block, lambda i: (0, 0, jnp.minimum(i, last), 0, 0)


def ring(first, order):
    def read(refs, k, part, g, late, shift):
        piece, position = order[k]
        return refs[first + piece][position, part, g]

    return read


def place(y, x, z):
    return (y % Y) * X * Z + (x % X) * Z + z


def moved(value, dy=0, dx=0, dz=0):
    perm = [
        (place(y + dy, x + dx, (z + dz) % Z), place(y, x, z))
        for y in range(Y)
        for x in range(X)
        for z in range(Z)
    ]
    return lax.ppermute(value, "sta", perm)


Z_GROUPS = [[place(y, x, z) for z in range(Z)] for y in range(Y) for x in range(X)]

RING = ((0, 0), (1, 0), (2, 0), (3, 0), (3, 2), (3, 1), (2, 1), (1, 1))


COLUMNS = (
    (0, 0, True),
    (1, 0, True),
    (0, 1, True),
    (0, 3, True),
    (1, 3, False),
    (1, 2, False),
    (1, 1, True),
    (0, 2, True),
)


def after(value, *others):
    return lax.optimization_barrier((value, *others))[0]


def per_device(traces, gaps, pair_mask):
    local = local_spectra(traces, gaps)
    own = lax.all_to_all(local, "frq", split_axis=0, concat_axis=0, tiled=True)[None]
    device = lax.axis_index("sta")
    y, x, z = device // (X * Z), device // Z % X, device % Z
    own_row = lax.dynamic_index_in_dim(pair_mask, device, 0, keepdims=False)
    scale = own_row.astype(jnp.float32).reshape(Y * X, Z) / WINDOWS
    turned = lax.dynamic_slice_in_dim(jnp.concatenate([scale, scale], 1), z, Z, 1)
    mask = jnp.repeat(jnp.concatenate([scale, turned], 0), STATIONS, 1)

    places = []
    for dy, dx, first in COLUMNS:
        column = (y + dy) % Y * X + (x + dx) % X
        places += [column, z, column + Y * X] if first else [column, 0 * z, column]
    where = jnp.stack(places).astype(jnp.int32)

    early = slice(None, GROUPS // 2)
    up1, down1 = moved(own, dz=1), moved(own, dz=-1)
    s01, s03 = moved(own, dx=1), moved(own, dx=-1)
    s10 = moved(own, dy=1)
    rows = own_rows(own[0])
    up1, down1 = lax.optimization_barrier((up1, down1, s10))[:2]
    up2, down2 = moved(up1, dz=1), moved(down1, dz=-1)
    s02 = moved(s01, dx=1)
    beside = moved(jnp.concatenate([s03, s01], 0), dy=1)
    s13, s11 = beside[:1], beside[1:]
    s12 = moved(s02, dy=1)
    near = jnp.concatenate([up1, down1], 0)
    n03 = moved(near, dx=-1)
    n01 = moved(after(near, s02), dx=1)
    n10 = moved(after(near, s12), dy=1)
    up3, down3 = moved(up2, dz=1), moved(down2, dz=-1)
    seeds = [s13, s12, s11[:, :, GROUPS // 2 :]]
    seeds = after(jnp.concatenate([seed.reshape(-1, 128) for seed in seeds], 0), up3, down3, n01, n03)
    far = lax.all_gather(seeds, "sta", axis_index_groups=Z_GROUPS)
    far = far.reshape(Z, 10, GROUPS, STATIONS, 128)
    low = moved(up3[:, :2], dz=1)
    high = moved(down3[:, 2:], dz=-1)
    middle = after(jnp.concatenate([up2, down2], 0), low, high, n10)
    m10, m01, m03 = moved(middle, dy=1), moved(middle, dx=1), moved(middle, dx=-1)
    last = jnp.concatenate([up3, down3, jnp.concatenate([low, high], 1)], 0)
    last = after(last, m01, m03, m10)
    l10, l01, l03 = moved(last, dy=1), moved(last, dx=1), moved(last, dx=-1)
    pieces = [whole(p) for p in (own, near, middle, last)]
    out = cross(None, 0, where, rows, mask, pieces, (ring(0, RING),))
    out, l01, l03 = lax.optimization_barrier((out, l01, l03))
    n11, m11, l11 = [moved(piece[:, :, early], dy=1) for piece in (n01, m01, l01)]
    c02 = [
        s02,
        moved(jnp.concatenate([n01, l01[2:]], 0), dx=1),
        moved(jnp.concatenate([m03, l03[:2]], 0), dx=-1),
    ]
    out = cross(
        out,
        1,
        where,
        rows,
        mask,
        [whole(p) for p in (s10, n10, m10, l10, s01, n01, m01, l01, s03, n03, m03, l03)],
        (ring(0, RING), ring(4, RING), ring(8, RING)),
    )
    columns = (Z, SLABS, GSTEP, STATIONS, 128)
    pieces = [(far, columns, lambda i, n=n: (0, n, i, 0, 0)) for n in range(2)]

    def gathered(n):
        return lambda refs, k, part, g, late, shift: refs[n][k, part, g]

    out = cross(
        out,
        4,
        where,
        rows,
        mask,
        pieces,
        (gathered(0), gathered(1)),
    )
    half = CROSS_STEPS // 2
    order = ((0, 0), (1, 0), (2, 0), (2, 2), (1, 2), (2, 3), (2, 1), (1, 1))
    pieces = [
        (far, (Z, 2, GSTEP, STATIONS, 128), lambda i: (0, SLABS, jnp.maximum(i - half, 0), 0, 0)),
        (far, (Z, 2, GSTEP, STATIONS, 128), lambda i: (0, SLABS, jnp.maximum(i, half), 0, 0)),
        *[whole(p) for p in (s11[:, :, early], n11, m11, l11, *c02)],
    ]

    def mixed(refs, k, part, g, late, shift):
        if late:
            return refs[part % 2][lax.rem(shift + k, Z), part // 2, g]
        return ring(2, RING)(refs, k, part, g, late, shift)

    return cross(
        out,
        6,
        where,
        rows,
        mask,
        pieces,
        (mixed, ring(6, order)),
        True,
    )


def solution(mesh):
    return jax.shard_map(
        per_device,
        mesh=mesh,
        in_specs=(P("sta", "frq", None), P("sta", "frq"), P()),
        out_specs=P(None, "sta", None, "frq"),
        check_vma=False,
    )
```

```python
import functools
import itertools
import math

import jax
import jax.numpy as jnp
import numpy as np
from jax import lax
from jax.experimental import pallas as pl
from jax.experimental.pallas import tpu as pltpu
from jax.sharding import PartitionSpec as P

SAMPLES = 4096
BINS = 512
HALF = 4
WINDOWS = 32
STATIONS = 16
LOCAL_WINDOWS = 8
SLABS = 4
SLAB_BINS = 128
GROUPS = 16
Y, X, Z = 2, 4, 8
COLUMN = Z * STATIONS
STEPS = 8
GSTEP = 8
CROSS_STEPS = GROUPS // GSTEP
VMEM_BYTES = 24 << 20
CROSS_VMEM_BYTES = 57 << 20


def basis_table():
    sample = np.arange(SAMPLES)
    bins = np.arange(1, BINS + 1)
    angle = (2.0 * math.pi / SAMPLES) * (sample[:, None] * bins[None, :] % SAMPLES)
    taper = 0.5 - 0.5 * np.cos((2.0 * math.pi / SAMPLES) * sample)
    scale = taper[:, None] / math.sqrt(SAMPLES)
    table = np.concatenate([scale * np.cos(angle), -scale * np.sin(angle)], 1)
    return table.astype(np.float32).astype(jnp.bfloat16)


def spectra_kernel(traces_ref, basis_ref, gaps_ref, out_ref, turned, traces_here, basis_here, done):
    rows = STATIONS * LOCAL_WINDOWS
    total = jnp.zeros((rows, 2 * BINS), jnp.float32)
    copies = [pltpu.make_async_copy(traces_ref, traces_here, done.at[STEPS])]
    parts = []
    for step in range(STEPS):
        depth = pl.ds(step * (SAMPLES // STEPS), SAMPLES // STEPS)
        parts.append(depth)
        copies.append(pltpu.make_async_copy(basis_ref.at[depth], basis_here.at[depth], done.at[step]))
    for copy in copies:
        copy.start()
    copies[0].wait()
    for depth, copy in zip(parts, copies[1:]):
        copy.wait()
        total += jnp.dot(traces_here[:, depth], basis_here[depth], preferred_element_type=jnp.float32)
    real = total[:, :BINS]
    imag = total[:, BINS:]
    magnitude = jnp.sqrt(real * real + imag * imag)
    lane = lax.broadcasted_iota(jnp.int32, magnitude.shape, 1)
    summed = magnitude
    for offset in range(1, HALF + 1):
        after = pltpu.roll(magnitude, BINS - offset, 1)
        before = pltpu.roll(magnitude, offset, 1)
        summed = summed + jnp.where(lane < BINS - offset, after, 0.0)
        summed = summed + jnp.where(lane >= offset, before, 0.0)
    counts = 1 + jnp.minimum(lane, HALF) + jnp.minimum(BINS - 1 - lane, HALF)
    smoothed = summed / counts.astype(jnp.float32)
    level = jnp.sum(magnitude, axis=1, keepdims=True) / BINS
    spread = jnp.concatenate([gaps_ref[...]] * STATIONS, 0)
    station = lax.broadcasted_iota(jnp.int32, spread.shape, 0) // LOCAL_WINDOWS
    chosen = station == lax.broadcasted_iota(jnp.int32, spread.shape, 1)
    complete = jnp.sum(jnp.where(chosen, spread, 0), axis=1, keepdims=True)
    factor = complete.astype(jnp.float32) / (smoothed + 0.1 * level + 1e-06)
    bins = lax.broadcasted_iota(jnp.int32, (BINS, BINS), 0)
    lanes = lax.broadcasted_iota(jnp.int32, (BINS, BINS), 1)
    order = (bins % 4 * 2 + bins // 4 % 2) * 64 + bins // 8 == lanes
    order = jnp.where(order, 1.0, 0.0).astype(jnp.bfloat16)
    parts = []
    for part in (real, imag):
        white = (part * factor).astype(jnp.bfloat16)
        parts.append(jnp.dot(white, order, preferred_element_type=jnp.float32))
    for station in range(STATIONS):
        at = slice(station * LOCAL_WINDOWS, (station + 1) * LOCAL_WINDOWS)
        stacked = jnp.concatenate(
            [parts[c][at, pair * 128 : pair * 128 + 128] for pair in range(4) for c in range(2)], 0
        )
        flipped = stacked.T
        joined = jnp.concatenate([flipped[:64], flipped[64:]], 1)
        turned[pl.ds(station, 64, stride=STATIONS), :] = joined
    out_ref[...] = turned[...].astype(jnp.bfloat16)


def local_spectra(traces, gaps):
    rows = STATIONS * LOCAL_WINDOWS
    flat = pl.pallas_call(
        spectra_kernel,
        out_shape=jax.ShapeDtypeStruct((SLABS * GROUPS * STATIONS, 128), jnp.bfloat16),
        in_specs=[
            pl.BlockSpec(memory_space=pl.ANY),
            pl.BlockSpec(memory_space=pl.ANY),
            pl.BlockSpec(memory_space=pltpu.VMEM),
        ],
        out_specs=pl.BlockSpec(memory_space=pltpu.VMEM),
        scratch_shapes=[
            pltpu.VMEM((SLABS * GROUPS * STATIONS, 128), jnp.float32),
            pltpu.VMEM((rows, SAMPLES), jnp.bfloat16),
            pltpu.VMEM((SAMPLES, 2 * BINS), jnp.bfloat16),
            pltpu.SemaphoreType.DMA((STEPS + 1,)),
        ],
        compiler_params=pltpu.CompilerParams(vmem_limit_bytes=60 << 20),
        cost_estimate=pl.CostEstimate(flops=1 << 30, bytes_accessed=10 << 20, transcendentals=0),
        name="spectra",
    )(traces.reshape(rows, SAMPLES), jnp.asarray(basis_table()), gaps.T)
    return flat.reshape(SLABS, GROUPS, STATIONS, 128)


def rows_kernel(own_ref, out_ref):
    for g, part in itertools.product(range(GSTEP), range(SLABS)):
        own = own_ref[part, g].astype(jnp.float32)
        lane = lax.broadcasted_iota(jnp.int32, own.shape, 1)
        real = lane // 8 % 2 == 0
        crossed = jnp.where(real, pltpu.roll(own, 120, 1), -pltpu.roll(own, 8, 1))
        for c, rows in enumerate((own, crossed)):
            spread = jnp.broadcast_to(rows[:, None, :], (STATIONS, 8, 128))
            j = lax.broadcasted_iota(jnp.int32, spread.shape, 1)
            owner = lax.broadcasted_iota(jnp.int32, spread.shape, 2) // 16
            spread = jnp.where(j == owner, spread, 0.0).reshape(128, 128)
            out_ref[pl.program_id(0) * GSTEP + g, c * 128 : c * 128 + 128, part * 128 : part * 128 + 128] = spread.astype(jnp.bfloat16)


def own_rows(own):
    return pl.pallas_call(
        rows_kernel,
        grid=(GROUPS // GSTEP,),
        out_shape=jax.ShapeDtypeStruct((GROUPS, 256, 512), jnp.bfloat16),
        in_specs=[pl.BlockSpec((SLABS, GSTEP, STATIONS, 128), lambda g: (0, g, 0, 0))],
        out_specs=pl.BlockSpec(memory_space=pltpu.VMEM),
        compiler_params=pltpu.CompilerParams(vmem_limit_bytes=VMEM_BYTES),
        cost_estimate=pl.CostEstimate(flops=1 << 22, bytes_accessed=5 << 20, transcendentals=0),
        name="own_rows",
    )(own)


def cross_kernel(base, columns, split, turned, where_ref, mask_ref, rows_ref, *refs):
    out_ref, products = refs[-2], refs[-1]
    step = pl.program_id(0)
    width = len(columns) * COLUMN

    def multiply(late):
        scale = jnp.concatenate([mask_ref[pl.ds(where_ref[3 * (base + n) + 2], 1), :] for n in range(len(columns))], 1)
        halves = []
        for g in range(GSTEP):
            others = jnp.concatenate(
                [
                    jnp.concatenate(
                        [
                            column(refs, k, part, g, late, where_ref[3 * (base + n) + 1])
                            for n, column in enumerate(columns)
                            for k in range(Z)
                        ],
                        0,
                    )
                    for part in range(SLABS)
                ],
                1,
            )
            product = lax.dot_general(
                rows_ref[step * GSTEP + g], others, (((1,), (1,)), ((), ())), preferred_element_type=jnp.float32
            )
            halves.append((product * scale).reshape(32, 8, width))
            if g % 2:
                first = pl.multiple_of(step * (GSTEP * 8) + (g - 1) * 8, 16)
                products[:, pl.ds(first, 16), :] = jnp.concatenate(halves, 1).astype(jnp.bfloat16)
                halves = []

    if split:
        pl.when(step < CROSS_STEPS // 2)(lambda: multiply(False))
        pl.when((step >= CROSS_STEPS // 2) & (step < CROSS_STEPS))(lambda: multiply(True))
    else:
        pl.when(step < CROSS_STEPS)(lambda: multiply(False))

    for n in range(len(columns)):

        @pl.when(step == CROSS_STEPS - 1 + n)
        def _():
            shift = where_ref[3 * (base + n) + 1]
            for c, a in itertools.product(range(2), range(STATIONS)):
                block = products[c * STATIONS + a, :, n * COLUMN : (n + 1) * COLUMN].T
                if not turned[n]:
                    out_ref[c, a] = block
                    continue
                for k in range(Z):
                    first = pl.multiple_of(lax.rem(shift + k, Z) * STATIONS, STATIONS)
                    out_ref[c, a, pl.ds(first, STATIONS), :] = block[k * STATIONS : k * STATIONS + STATIONS]


def cross(out, base, where, rows, mask, pieces, columns, split=False):
    def number(i, w):
        return w[3 * (base + jnp.maximum(i - (CROSS_STEPS - 1), 0))]

    in_specs = [pl.BlockSpec(memory_space=pltpu.VMEM), pl.BlockSpec(memory_space=pltpu.VMEM)]
    for _, block, at in pieces:
        in_specs.append(pl.BlockSpec(block, lambda i, w, at=at: at(jnp.minimum(i, CROSS_STEPS - 1))))
    args = [where, mask, rows, *[piece for piece, _, _ in pieces]]
    aliases = {}
    if out is not None:
        in_specs.append(pl.BlockSpec(memory_space=pl.ANY))
        aliases = {len(args): 0}
        args.append(out)
    stations = Y * X * COLUMN
    n = len(columns)
    turned = [first for _, _, first in COLUMNS[base : base + n]]
    return pl.pallas_call(
        functools.partial(cross_kernel, base, columns, split, turned),
        grid_spec=pltpu.PrefetchScalarGridSpec(
            num_scalar_prefetch=1,
            grid=(CROSS_STEPS + n - 1,),
            in_specs=in_specs,
            out_specs=pl.BlockSpec((2, STATIONS, COLUMN, SLAB_BINS), lambda i, w: (0, 0, number(i, w), 0)),
            scratch_shapes=[pltpu.VMEM((2 * STATIONS, SLAB_BINS, n * COLUMN), jnp.bfloat16)],
        ),
        out_shape=jax.ShapeDtypeStruct((2, STATIONS, stations, SLAB_BINS), jnp.bfloat16),
        input_output_aliases=aliases,
        compiler_params=pltpu.CompilerParams(vmem_limit_bytes=CROSS_VMEM_BYTES),
        cost_estimate=pl.CostEstimate(
            flops=n << 29, bytes_accessed=1, transcendentals=0
        ),
        name="cross",
    )(*args)


def whole(piece):
    block = (piece.shape[0], SLABS, GSTEP, STATIONS, 128)
    last = piece.shape[2] // GSTEP - 1
    return piece, block, lambda i: (0, 0, jnp.minimum(i, last), 0, 0)


def ring(first, order):
    def read(refs, k, part, g, late, shift):
        piece, position = order[k]
        return refs[first + piece][position, part, g]

    return read


def place(y, x, z):
    return (y % Y) * X * Z + (x % X) * Z + z


def moved(value, dy=0, dx=0, dz=0):
    perm = [
        (place(y + dy, x + dx, (z + dz) % Z), place(y, x, z))
        for y in range(Y)
        for x in range(X)
        for z in range(Z)
    ]
    return lax.ppermute(value, "sta", perm)


Z_GROUPS = [[place(y, x, z) for z in range(Z)] for y in range(Y) for x in range(X)]

RING = ((0, 0), (1, 0), (2, 0), (3, 0), (3, 2), (3, 1), (2, 1), (1, 1))


COLUMNS = (
    (0, 0, True),
    (1, 0, True),
    (0, 1, True),
    (0, 3, True),
    (1, 3, False),
    (1, 2, False),
    (1, 1, True),
    (0, 2, True),
)


def after(value, *others):
    return lax.optimization_barrier((value, *others))[0]


def per_device(traces, gaps, pair_mask):
    local = local_spectra(traces, gaps)
    own = lax.all_to_all(local, "frq", split_axis=0, concat_axis=0, tiled=True)[None]
    device = lax.axis_index("sta")
    y, x, z = device // (X * Z), device // Z % X, device % Z
    own_row = lax.dynamic_index_in_dim(pair_mask, device, 0, keepdims=False)
    scale = own_row.astype(jnp.float32).reshape(Y * X, Z) / WINDOWS
    turned = lax.dynamic_slice_in_dim(jnp.concatenate([scale, scale], 1), z, Z, 1)
    mask = jnp.repeat(jnp.concatenate([scale, turned], 0), STATIONS, 1)

    places = []
    for dy, dx, first in COLUMNS:
        column = (y + dy) % Y * X + (x + dx) % X
        places += [column, z, column + Y * X] if first else [column, 0 * z, column]
    where = jnp.stack(places).astype(jnp.int32)

    early = slice(None, GROUPS // 2)
    up1, down1 = moved(own, dz=1), moved(own, dz=-1)
    s01, s03 = moved(own, dx=1), moved(own, dx=-1)
    s10 = moved(own, dy=1)
    rows = own_rows(own[0])
    up1, down1 = lax.optimization_barrier((up1, down1, s10))[:2]
    up2, down2 = moved(up1, dz=1), moved(down1, dz=-1)
    s02 = moved(s01, dx=1)
    beside = moved(jnp.concatenate([s03, s01], 0), dy=1)
    s13, s11 = beside[:1], beside[1:]
    s12 = moved(s02, dy=1)
    near = jnp.concatenate([up1, down1], 0)
    n03 = moved(near, dx=-1)
    n01 = moved(after(near, s02), dx=1)
    n10 = moved(after(near, s12), dy=1)
    up3, down3 = moved(up2, dz=1), moved(down2, dz=-1)
    seeds = [s13, s12, s11[:, :, GROUPS // 2 :]]
    seeds = after(jnp.concatenate([seed.reshape(-1, 128) for seed in seeds], 0), up3, down3, n01, n03)
    far = lax.all_gather(seeds, "sta", axis_index_groups=Z_GROUPS)
    far = far.reshape(Z, 10, GROUPS, STATIONS, 128)
    low = moved(up3[:, :2], dz=1)
    high = moved(down3[:, 2:], dz=-1)
    middle = after(jnp.concatenate([up2, down2], 0), low, high, n10)
    m10, m01, m03 = moved(middle, dy=1), moved(middle, dx=1), moved(middle, dx=-1)
    last = jnp.concatenate([up3, down3, jnp.concatenate([low, high], 1)], 0)
    last = after(last, m01, m03, m10)
    l10, l01, l03 = moved(last, dy=1), moved(last, dx=1), moved(last, dx=-1)
    pieces = [whole(p) for p in (own, near, middle, last)]
    out = cross(None, 0, where, rows, mask, pieces, (ring(0, RING),))
    out, l01, l03 = lax.optimization_barrier((out, l01, l03))
    n11, m11, l11 = [moved(piece[:, :, early], dy=1) for piece in (n01, m01, l01)]
    c02 = [
        s02,
        moved(jnp.concatenate([n01, l01[2:]], 0), dx=1),
        moved(jnp.concatenate([m03, l03[:2]], 0), dx=-1),
    ]
    out = cross(
        out,
        1,
        where,
        rows,
        mask,
        [whole(p) for p in (s10, n10, m10, l10, s01, n01, m01, l01, s03, n03, m03, l03)],
        (ring(0, RING), ring(4, RING), ring(8, RING)),
    )
    columns = (Z, SLABS, GSTEP, STATIONS, 128)
    pieces = [(far, columns, lambda i, n=n: (0, n, i, 0, 0)) for n in range(2)]

    def gathered(n):
        return lambda refs, k, part, g, late, shift: refs[n][k, part, g]

    out = cross(
        out,
        4,
        where,
        rows,
        mask,
        pieces,
        (gathered(0), gathered(1)),
    )
    half = CROSS_STEPS // 2
    order = ((0, 0), (1, 0), (2, 0), (2, 2), (1, 2), (2, 3), (2, 1), (1, 1))
    pieces = [
        (far, (Z, 2, GSTEP, STATIONS, 128), lambda i: (0, SLABS, jnp.maximum(i - half, 0), 0, 0)),
        (far, (Z, 2, GSTEP, STATIONS, 128), lambda i: (0, SLABS, jnp.maximum(i, half), 0, 0)),
        *[whole(p) for p in (s11[:, :, early], n11, m11, l11, *c02)],
    ]

    def mixed(refs, k, part, g, late, shift):
        if late:
            return refs[part % 2][lax.rem(shift + k, Z), part // 2, g]
        return ring(2, RING)(refs, k, part, g, late, shift)

    return cross(
        out,
        6,
        where,
        rows,
        mask,
        pieces,
        (mixed, ring(6, order)),
        True,
    )


def solution(mesh):
    return jax.shard_map(
        per_device,
        mesh=mesh,
        in_specs=(P("sta", "frq", None), P("sta", "frq"), P()),
        out_specs=P(None, "sta", None, "frq"),
        check_vma=False,
    )
```

```python
import functools
import itertools
import math

import jax
import jax.numpy as jnp
import numpy as np
from jax import lax
from jax.experimental import pallas as pl
from jax.experimental.pallas import tpu as pltpu
from jax.sharding import PartitionSpec as P

SAMPLES = 4096
BINS = 512
HALF = 4
WINDOWS = 32
STATIONS = 16
LOCAL_WINDOWS = 8
SLABS = 4
SLAB_BINS = 128
GROUPS = 16
Y, X, Z = 2, 4, 8
COLUMN = Z * STATIONS
STEPS = 8
GSTEP = 8
CROSS_STEPS = GROUPS // GSTEP
VMEM_BYTES = 24 << 20
CROSS_VMEM_BYTES = 57 << 20


def basis_table():
    sample = np.arange(SAMPLES)
    bins = np.arange(1, BINS + 1)
    angle = (2.0 * math.pi / SAMPLES) * (sample[:, None] * bins[None, :] % SAMPLES)
    taper = 0.5 - 0.5 * np.cos((2.0 * math.pi / SAMPLES) * sample)
    scale = taper[:, None] / math.sqrt(SAMPLES)
    table = np.concatenate([scale * np.cos(angle), -scale * np.sin(angle)], 1)
    return table.astype(np.float32).astype(jnp.bfloat16)


def spectra_kernel(traces_ref, basis_ref, gaps_ref, out_ref, turned, traces_here, basis_here, done):
    rows = STATIONS * LOCAL_WINDOWS
    total = jnp.zeros((rows, 2 * BINS), jnp.float32)
    copies = [pltpu.make_async_copy(traces_ref, traces_here, done.at[STEPS])]
    parts = []
    for step in range(STEPS):
        depth = pl.ds(step * (SAMPLES // STEPS), SAMPLES // STEPS)
        parts.append(depth)
        copies.append(pltpu.make_async_copy(basis_ref.at[depth], basis_here.at[depth], done.at[step]))
    for copy in copies:
        copy.start()
    copies[0].wait()
    for depth, copy in zip(parts, copies[1:]):
        copy.wait()
        total += jnp.dot(traces_here[:, depth], basis_here[depth], preferred_element_type=jnp.float32)
    real = total[:, :BINS]
    imag = total[:, BINS:]
    magnitude = jnp.sqrt(real * real + imag * imag)
    lane = lax.broadcasted_iota(jnp.int32, magnitude.shape, 1)
    summed = magnitude
    for offset in range(1, HALF + 1):
        after = pltpu.roll(magnitude, BINS - offset, 1)
        before = pltpu.roll(magnitude, offset, 1)
        summed = summed + jnp.where(lane < BINS - offset, after, 0.0)
        summed = summed + jnp.where(lane >= offset, before, 0.0)
    counts = 1 + jnp.minimum(lane, HALF) + jnp.minimum(BINS - 1 - lane, HALF)
    smoothed = summed / counts.astype(jnp.float32)
    level = jnp.sum(magnitude, axis=1, keepdims=True) / BINS
    spread = jnp.concatenate([gaps_ref[...]] * STATIONS, 0)
    station = lax.broadcasted_iota(jnp.int32, spread.shape, 0) // LOCAL_WINDOWS
    chosen = station == lax.broadcasted_iota(jnp.int32, spread.shape, 1)
    complete = jnp.sum(jnp.where(chosen, spread, 0), axis=1, keepdims=True)
    factor = complete.astype(jnp.float32) / (smoothed + 0.1 * level + 1e-06)
    bins = lax.broadcasted_iota(jnp.int32, (BINS, BINS), 0)
    lanes = lax.broadcasted_iota(jnp.int32, (BINS, BINS), 1)
    order = (bins % 4 * 2 + bins // 4 % 2) * 64 + bins // 8 == lanes
    order = jnp.where(order, 1.0, 0.0).astype(jnp.bfloat16)
    parts = []
    for part in (real, imag):
        white = (part * factor).astype(jnp.bfloat16)
        parts.append(jnp.dot(white, order, preferred_element_type=jnp.float32))
    for station in range(STATIONS):
        at = slice(station * LOCAL_WINDOWS, (station + 1) * LOCAL_WINDOWS)
        stacked = jnp.concatenate(
            [parts[c][at, pair * 128 : pair * 128 + 128] for pair in range(4) for c in range(2)], 0
        )
        flipped = stacked.T
        joined = jnp.concatenate([flipped[:64], flipped[64:]], 1)
        turned[pl.ds(station, 64, stride=STATIONS), :] = joined
    out_ref[...] = turned[...].astype(jnp.bfloat16)


def local_spectra(traces, gaps):
    rows = STATIONS * LOCAL_WINDOWS
    flat = pl.pallas_call(
        spectra_kernel,
        out_shape=jax.ShapeDtypeStruct((SLABS * GROUPS * STATIONS, 128), jnp.bfloat16),
        in_specs=[
            pl.BlockSpec(memory_space=pl.ANY),
            pl.BlockSpec(memory_space=pl.ANY),
            pl.BlockSpec(memory_space=pltpu.VMEM),
        ],
        out_specs=pl.BlockSpec(memory_space=pltpu.VMEM),
        scratch_shapes=[
            pltpu.VMEM((SLABS * GROUPS * STATIONS, 128), jnp.float32),
            pltpu.VMEM((rows, SAMPLES), jnp.bfloat16),
            pltpu.VMEM((SAMPLES, 2 * BINS), jnp.bfloat16),
            pltpu.SemaphoreType.DMA((STEPS + 1,)),
        ],
        compiler_params=pltpu.CompilerParams(vmem_limit_bytes=60 << 20),
        cost_estimate=pl.CostEstimate(flops=1 << 30, bytes_accessed=10 << 20, transcendentals=0),
        name="spectra",
    )(traces.reshape(rows, SAMPLES), jnp.asarray(basis_table()), gaps.T)
    return flat.reshape(SLABS, GROUPS, STATIONS, 128)


def rows_kernel(own_ref, out_ref):
    for g, part in itertools.product(range(GSTEP), range(SLABS)):
        own = own_ref[part, g].astype(jnp.float32)
        lane = lax.broadcasted_iota(jnp.int32, own.shape, 1)
        real = lane // 8 % 2 == 0
        crossed = jnp.where(real, pltpu.roll(own, 120, 1), -pltpu.roll(own, 8, 1))
        for c, rows in enumerate((own, crossed)):
            spread = jnp.broadcast_to(rows[:, None, :], (STATIONS, 8, 128))
            j = lax.broadcasted_iota(jnp.int32, spread.shape, 1)
            owner = lax.broadcasted_iota(jnp.int32, spread.shape, 2) // 16
            spread = jnp.where(j == owner, spread, 0.0).reshape(128, 128)
            out_ref[pl.program_id(0) * GSTEP + g, c * 128 : c * 128 + 128, part * 128 : part * 128 + 128] = spread.astype(jnp.bfloat16)


def own_rows(own):
    return pl.pallas_call(
        rows_kernel,
        grid=(GROUPS // GSTEP,),
        out_shape=jax.ShapeDtypeStruct((GROUPS, 256, 512), jnp.bfloat16),
        in_specs=[pl.BlockSpec((SLABS, GSTEP, STATIONS, 128), lambda g: (0, g, 0, 0))],
        out_specs=pl.BlockSpec(memory_space=pltpu.VMEM),
        compiler_params=pltpu.CompilerParams(vmem_limit_bytes=VMEM_BYTES),
        cost_estimate=pl.CostEstimate(flops=1 << 22, bytes_accessed=5 << 20, transcendentals=0),
        name="own_rows",
    )(own)


def cross_kernel(base, columns, split, turned, where_ref, mask_ref, rows_ref, *refs):
    out_ref, products = refs[-2], refs[-1]
    step = pl.program_id(0)
    width = len(columns) * COLUMN

    def multiply(late):
        scale = jnp.concatenate([mask_ref[pl.ds(where_ref[3 * (base + n) + 2], 1), :] for n in range(len(columns))], 1)
        halves = []
        for g in range(GSTEP):
            others = jnp.concatenate(
                [
                    jnp.concatenate(
                        [
                            column(refs, k, part, g, late, where_ref[3 * (base + n) + 1])
                            for n, column in enumerate(columns)
                            for k in range(Z)
                        ],
                        0,
                    )
                    for part in range(SLABS)
                ],
                1,
            )
            product = lax.dot_general(
                rows_ref[step * GSTEP + g], others, (((1,), (1,)), ((), ())), preferred_element_type=jnp.float32
            )
            halves.append((product * scale).reshape(32, 8, width))
            if g % 2:
                first = pl.multiple_of(step * (GSTEP * 8) + (g - 1) * 8, 16)
                products[:, pl.ds(first, 16), :] = jnp.concatenate(halves, 1).astype(jnp.bfloat16)
                halves = []

    if split:
        pl.when(step < CROSS_STEPS // 2)(lambda: multiply(False))
        pl.when((step >= CROSS_STEPS // 2) & (step < CROSS_STEPS))(lambda: multiply(True))
    else:
        pl.when(step < CROSS_STEPS)(lambda: multiply(False))

    for n in range(len(columns)):

        @pl.when(step == CROSS_STEPS - 1 + n)
        def _():
            shift = where_ref[3 * (base + n) + 1]
            for c, a in itertools.product(range(2), range(STATIONS)):
                block = products[c * STATIONS + a, :, n * COLUMN : (n + 1) * COLUMN].T
                if not turned[n]:
                    out_ref[c, a] = block
                    continue
                for k in range(Z):
                    first = pl.multiple_of(lax.rem(shift + k, Z) * STATIONS, STATIONS)
                    out_ref[c, a, pl.ds(first, STATIONS), :] = block[k * STATIONS : k * STATIONS + STATIONS]


def cross(out, base, where, rows, mask, pieces, columns, split=False):
    def number(i, w):
        return w[3 * (base + jnp.maximum(i - (CROSS_STEPS - 1), 0))]

    in_specs = [pl.BlockSpec(memory_space=pltpu.VMEM), pl.BlockSpec(memory_space=pltpu.VMEM)]
    for _, block, at in pieces:
        in_specs.append(pl.BlockSpec(block, lambda i, w, at=at: at(jnp.minimum(i, CROSS_STEPS - 1))))
    args = [where, mask, rows, *[piece for piece, _, _ in pieces]]
    aliases = {}
    if out is not None:
        in_specs.append(pl.BlockSpec(memory_space=pl.ANY))
        aliases = {len(args): 0}
        args.append(out)
    stations = Y * X * COLUMN
    n = len(columns)
    turned = [first for _, _, first in COLUMNS[base : base + n]]
    return pl.pallas_call(
        functools.partial(cross_kernel, base, columns, split, turned),
        grid_spec=pltpu.PrefetchScalarGridSpec(
            num_scalar_prefetch=1,
            grid=(CROSS_STEPS + n - 1,),
            in_specs=in_specs,
            out_specs=pl.BlockSpec((2, STATIONS, COLUMN, SLAB_BINS), lambda i, w: (0, 0, number(i, w), 0)),
            scratch_shapes=[pltpu.VMEM((2 * STATIONS, SLAB_BINS, n * COLUMN), jnp.bfloat16)],
        ),
        out_shape=jax.ShapeDtypeStruct((2, STATIONS, stations, SLAB_BINS), jnp.bfloat16),
        input_output_aliases=aliases,
        compiler_params=pltpu.CompilerParams(vmem_limit_bytes=CROSS_VMEM_BYTES),
        cost_estimate=pl.CostEstimate(
            flops=n << 29, bytes_accessed=1, transcendentals=0
        ),
        name="cross",
    )(*args)


def whole(piece):
    block = (piece.shape[0], SLABS, GSTEP, STATIONS, 128)
    last = piece.shape[2] // GSTEP - 1
    return piece, block, lambda i: (0, 0, jnp.minimum(i, last), 0, 0)


def ring(first, order):
    def read(refs, k, part, g, late, shift):
        piece, position = order[k]
        return refs[first + piece][position, part, g]

    return read


def place(y, x, z):
    return (y % Y) * X * Z + (x % X) * Z + z


def moved(value, dy=0, dx=0, dz=0):
    perm = [
        (place(y + dy, x + dx, (z + dz) % Z), place(y, x, z))
        for y in range(Y)
        for x in range(X)
        for z in range(Z)
    ]
    return lax.ppermute(value, "sta", perm)


Z_GROUPS = [[place(y, x, z) for z in range(Z)] for y in range(Y) for x in range(X)]

RING = ((0, 0), (1, 0), (2, 0), (3, 0), (3, 2), (3, 1), (2, 1), (1, 1))


COLUMNS = (
    (0, 0, True),
    (1, 0, True),
    (0, 1, True),
    (0, 3, True),
    (1, 3, False),
    (1, 2, False),
    (1, 1, True),
    (0, 2, True),
)


def after(value, *others):
    return lax.optimization_barrier((value, *others))[0]


def per_device(traces, gaps, pair_mask):
    local = local_spectra(traces, gaps)
    own = lax.all_to_all(local, "frq", split_axis=0, concat_axis=0, tiled=True)[None]
    device = lax.axis_index("sta")
    y, x, z = device // (X * Z), device // Z % X, device % Z
    own_row = lax.dynamic_index_in_dim(pair_mask, device, 0, keepdims=False)
    scale = own_row.astype(jnp.float32).reshape(Y * X, Z) / WINDOWS
    turned = lax.dynamic_slice_in_dim(jnp.concatenate([scale, scale], 1), z, Z, 1)
    mask = jnp.repeat(jnp.concatenate([scale, turned], 0), STATIONS, 1)

    places = []
    for dy, dx, first in COLUMNS:
        column = (y + dy) % Y * X + (x + dx) % X
        places += [column, z, column + Y * X] if first else [column, 0 * z, column]
    where = jnp.stack(places).astype(jnp.int32)

    early = slice(None, GROUPS // 2)
    up1, down1 = moved(own, dz=1), moved(own, dz=-1)
    s01, s03 = moved(own, dx=1), moved(own, dx=-1)
    s10 = moved(own, dy=1)
    rows = own_rows(own[0])
    up1, down1 = lax.optimization_barrier((up1, down1, s10))[:2]
    up2, down2 = moved(up1, dz=1), moved(down1, dz=-1)
    s02 = moved(s01, dx=1)
    beside = moved(jnp.concatenate([s03, s01], 0), dy=1)
    s13, s11 = beside[:1], beside[1:]
    s12 = moved(s02, dy=1)
    near = jnp.concatenate([up1, down1], 0)
    n03 = moved(near, dx=-1)
    n01 = moved(after(near, s02), dx=1)
    n10 = moved(after(near, s12), dy=1)
    up3, down3 = moved(up2, dz=1), moved(down2, dz=-1)
    seeds = [s13, s12, s11[:, :, GROUPS // 2 :]]
    seeds = after(jnp.concatenate([seed.reshape(-1, 128) for seed in seeds], 0), up3, down3, n01, n03)
    far = lax.all_gather(seeds, "sta", axis_index_groups=Z_GROUPS)
    far = far.reshape(Z, 10, GROUPS, STATIONS, 128)
    low = moved(up3[:, :2], dz=1)
    high = moved(down3[:, 2:], dz=-1)
    middle = after(jnp.concatenate([up2, down2], 0), low, high, n10)
    m10, m01, m03 = moved(middle, dy=1), moved(middle, dx=1), moved(middle, dx=-1)
    last = jnp.concatenate([up3, down3, jnp.concatenate([low, high], 1)], 0)
    last = after(last, m01, m03, m10)
    l10, l01, l03 = moved(last, dy=1), moved(last, dx=1), moved(last, dx=-1)
    pieces = [whole(p) for p in (own, near, middle, last)]
    out = cross(None, 0, where, rows, mask, pieces, (ring(0, RING),))
    out, l01, l03 = lax.optimization_barrier((out, l01, l03))
    n11 = moved(n01[:, :, early], dy=1)
    l11 = moved(jnp.concatenate([m01[:, :, early], l01[:, :, early]], 0), dy=1)
    c02 = [
        s02,
        moved(jnp.concatenate([n01, l01[2:]], 0), dx=1),
        moved(jnp.concatenate([m03, l03[:2]], 0), dx=-1),
    ]
    out = cross(
        out,
        1,
        where,
        rows,
        mask,
        [whole(p) for p in (s10, n10, m10, l10, s01, n01, m01, l01, s03, n03, m03, l03)],
        (ring(0, RING), ring(4, RING), ring(8, RING)),
    )
    columns = (Z, SLABS, GSTEP, STATIONS, 128)
    pieces = [(far, columns, lambda i, n=n: (0, n, i, 0, 0)) for n in range(2)]

    def gathered(n):
        return lambda refs, k, part, g, late, shift: refs[n][k, part, g]

    out = cross(
        out,
        4,
        where,
        rows,
        mask,
        pieces,
        (gathered(0), gathered(1)),
    )
    half = CROSS_STEPS // 2
    order = ((0, 0), (1, 0), (2, 0), (2, 2), (1, 2), (2, 3), (2, 1), (1, 1))
    merged = ((0, 0), (1, 0), (2, 0), (2, 2), (2, 4), (2, 3), (2, 1), (1, 1))
    pieces = [
        (far, (Z, 2, GSTEP, STATIONS, 128), lambda i: (0, SLABS, jnp.maximum(i - half, 0), 0, 0)),
        (far, (Z, 2, GSTEP, STATIONS, 128), lambda i: (0, SLABS, jnp.maximum(i, half), 0, 0)),
        *[whole(p) for p in (s11[:, :, early], n11, l11, *c02)],
    ]

    def mixed(refs, k, part, g, late, shift):
        if late:
            return refs[part % 2][lax.rem(shift + k, Z), part // 2, g]
        return ring(2, merged)(refs, k, part, g, late, shift)

    return cross(
        out,
        6,
        where,
        rows,
        mask,
        pieces,
        (mixed, ring(5, order)),
        True,
    )


def solution(mesh):
    return jax.shard_map(
        per_device,
        mesh=mesh,
        in_specs=(P("sta", "frq", None), P("sta", "frq"), P()),
        out_specs=P(None, "sta", None, "frq"),
        check_vma=False,
    )
```
